32 devices in a mesh: horiz: 8 (over z, y), lev: 4 (over x, core).
Axes of the slice: x: 2, y: 2, z: 4, core: 2. Of those that a mesh axis runs over, the one named last changes fastest.
Arguments:
- control: float32 [64, 32, 4096], P('lev', None, 'horiz'), may hold values from -6 to 6
- members: bfloat16 [64, 4, 32, 4096], P('lev', None, None, 'horiz'), may hold values from -6 to 6
- extinction: float32 [4], replicated, may hold values from 0.5 to 2
- kernels: bfloat16 [4096, 64, 128], P('horiz', 'lev'), may hold values from 0 to 1
- innovation: bfloat16 [4096, 128], P('horiz'), may hold values from -16 to 16
- obs_weight: bfloat16 [4096, 128], P('horiz'), may hold values from 0.25 to 4
- owners: int32 [4096, 1], P('horiz'), may hold values from 0 to 7; in each aligned block of 512 rows (0 to 511, 512 to 1023, ...) at most 128 rows name the same one
- pixel_columns: int32 [4096, 128], P('horiz'), may hold values from 0 to 511
- pixel_counts: int32 [4096], P('horiz'), may hold values from 1 to 128
Outputs:
- gradient: float32 [64, 32, 4096], P('lev', None, 'horiz')
The draws below stay inside these ranges and needn't reach their ends.
Inputs may be any that keep to these rules, and one draw needn't show every extreme that they name: `owners`: among the 512 blocks of one index of horiz, no owner is named more than 128 times, and in some index's blocks one owner is named exactly 128 times.
All inputs are finite; a program needn't handle non-finite values.
Results may differ from the reference program's by a relative error of at most 0.0037.
Values may be sent and summed in bfloat16 or wider, within the bound.
A program may use at most 128 MiB of HBM per device.

```python
import math
import jax
import jax.numpy as jnp
import numpy as np
from jax import lax

LEV = 64
SPEC = 4
MEM = 32
BLK = 128
HALF = 4
COL_DEV = 512
OBS_DEV = 512
NCOL = 4096
NBLK = 4096
CAP = 128
N_HORIZ = 8


def set_ends(values, rng, smallest, top_value):
    index_at = [jax.random.randint(jax.random.fold_in(rng, axis), (), 0, length) for axis, length in enumerate(values.shape)]
    widest = values.shape.index(max(values.shape))
    neighbour = index_at[:widest] + [(index_at[widest] + 1) % values.shape[widest]] + index_at[widest + 1:]
    return values.at[tuple(index_at)].set(smallest).at[tuple(neighbour)].set(top_value)


def levels(key, shape, split, least, high):
    factor_of, own = 1.0, jax.random.fold_in(key, 6)
    for position, parts in split:
        steps = jnp.exp(jax.random.uniform(jax.random.fold_in(own, position), (parts,), jnp.float32, least / len(split), high / len(split)))
        factor_of = factor_of * jnp.repeat(steps, shape[position] // parts).reshape([-1 if axis == position else 1 for axis in range(len(shape))])
    return factor_of


def shared_out(own_key, own, number, rows, count, top, limit, skew):
    order = jax.random.permutation(own_key, count)
    crowded, common = portions_of(count, rows * top, limit, skew, True), portions_of(count, rows * top, limit, skew, False)
    places = jnp.arange(count)

    def named(lengths, rotation):
        used = int((lengths > 0).sum())
        fixed = max(1, used // 4)
        moved = fixed + (places - fixed + rotation * (used - fixed)) % max(1, count - fixed)
        return jnp.zeros((count,), jnp.int32).at[order[jnp.where(places < fixed, places, moved)]].set(jnp.asarray(lengths, jnp.int32))

    lengths = jnp.where(number % 4 == 0, named(crowded, number // 4), named(common, number - number // 4 - 1))
    mixed = jax.random.permutation(jax.random.fold_in(own, 3), count)
    donor, taker = mixed[0:count // 2 * 2:2], mixed[1:count // 2 * 2:2]
    slack = jnp.minimum(lengths[donor] - 1, limit - lengths[taker]) // 2
    slack = jnp.where((donor == order[0]) | (taker == order[0]) | (lengths[taker] == 0), 0, jnp.maximum(slack, 0))
    moved = jax.random.randint(jax.random.fold_in(own, 4), (count // 2,), 0, 1 << 20) % (slack + 1)
    lengths = lengths.at[donor].add(-moved).at[taker].add(moved)
    labels = jnp.searchsorted(jnp.cumsum(lengths), jnp.arange(rows * top), side="right").astype(jnp.int32)
    table = labels.reshape(top, rows).T
    table = table[jax.random.permutation(jax.random.fold_in(own, 1), rows)]
    rotation = jax.random.randint(jax.random.fold_in(own, 2), (rows, 1), 0, top)
    return jnp.take_along_axis(table, (jnp.arange(top)[None, :] + rotation) % top, axis=1)


def portions_of(count, total, reach, skew, full):
    loads = [(1 << 20) // math.isqrt(grade ** skew) + 1 for grade in range(1, count + 1)]
    largest = reach if full else min(reach, max(-(-total // count), total * loads[0] // sum(loads)))
    least = 1 if total - largest >= count - 1 else 0
    given, surplus = [largest] + [least] * (count - 1), total - largest - least * (count - 1)
    while surplus > 0:
        candidates = [i for i in range(1, count) if given[i] < largest] or [i for i in range(1, count) if given[i] < reach]
        pool, remaining = sum([loads[i] for i in candidates]), surplus
        for i in candidates:
            more = min(reach - given[i], max(1, remaining * loads[i] // pool), surplus)
            given[i] = given[i] + more
            surplus = surplus - more
    return np.array(given)


def centred(own_key, extent, scale, limit, pieces=(), held_as=jnp.bfloat16):
    values = scale * jax.random.normal(own_key, extent, jnp.float32)
    if pieces:
        values = values * levels(own_key, extent, pieces, -0.22, 0.18)
    return jnp.clip(values, -limit, limit).astype(held_as)


def setup_inputs(seed: int = 0) -> dict:
    streams_of = jax.random.split(jax.random.key(seed), 10)
    control = centred(streams_of[0], (LEV, MEM, NCOL), 1.0, 6.0, ((0, 4), (2, 8)), jnp.float32)
    members = centred(streams_of[1], (LEV, SPEC, MEM, NCOL), 1.0, 6.0, ((0, 4), (3, 8)))
    extinction = jnp.clip(jnp.exp(jax.random.uniform(streams_of[2], (SPEC,), jnp.float32, math.log(0.5), math.log(2.0))), 0.5, 2.0)
    kernels = jnp.clip(1.0 * jax.random.uniform(streams_of[3], (NBLK, LEV, BLK), jnp.float32) ** levels(streams_of[3], (NBLK, LEV, BLK), ((0, 8), (1, 4)), -0.2, 0.2), 0.0, 1.0).astype(jnp.bfloat16)
    innovation = centred(streams_of[4], (NBLK, BLK), 3.0, 16.0, ((0, 8),))
    obs_weight = jnp.clip(jnp.exp(math.log(4.0) - 2.7725887 * jax.random.uniform(streams_of[5], (NBLK, BLK), jnp.float32) ** levels(streams_of[5], (NBLK, BLK), ((0, 8),), -0.2, 0.2)), 0.25, 4.0).astype(jnp.bfloat16)
    owners_keys = jax.random.split(jax.random.fold_in(streams_of[6], 1), NBLK // OBS_DEV)
    owners_turns = jax.random.permutation(jax.random.fold_in(streams_of[6], 3), NBLK // OBS_DEV)
    owners = jax.vmap(lambda own, number: shared_out(jax.random.fold_in(streams_of[6], 2), own, number, OBS_DEV, N_HORIZ, 1, CAP, 2))(owners_keys, owners_turns).reshape((NBLK, 1))
    pixel_columns = set_ends(jax.random.randint(streams_of[7], (NBLK, BLK), 0, COL_DEV), jax.random.fold_in(streams_of[7], 1), 0, COL_DEV - 1).astype(jnp.int32)
    pixel_counts = set_ends(jax.random.randint(streams_of[8], (NBLK,), 1, BLK + 1), jax.random.fold_in(streams_of[8], 1), 1, BLK).astype(jnp.int32)
    return {"control": control, "members": members, "extinction": extinction, "kernels": kernels, "innovation": innovation, "obs_weight": obs_weight, "owners": owners, "pixel_columns": pixel_columns, "pixel_counts": pixel_counts}


def level_matrix():
    index_levels = jnp.arange(LEV, dtype=jnp.float32)
    spread = LEV / 8.0
    distance = index_levels[:, None] - index_levels[None, :]
    matrix = jnp.exp(-distance * distance / (2.0 * spread * spread)) / (2.5066283 * spread)
    return matrix.astype(jnp.bfloat16)

def column_taps():
    offsets = jnp.arange(2 * HALF + 1, dtype=jnp.float32) - HALF
    spread = HALF / 2.0
    weights = jnp.exp(-offsets * offsets / (2.0 * spread * spread))
    return weights / jnp.sum(weights)

def smooth_columns(values):
    tap_weights = column_taps()
    span = values.shape[2]
    padded = jnp.pad(values, ((0, 0), (0, 0), (HALF, HALF)))
    running = jnp.zeros(values.shape, jnp.float32)
    for offset in range(2 * HALF + 1):
        running = running + tap_weights[offset] * padded[:, :, offset:offset + span]
    return running

def reference(control, members, extinction, kernels, innovation, obs_weight, owners, pixel_columns, pixel_counts):
    level_loc = level_matrix().astype(jnp.float32)
    scale = 1.0 / math.sqrt(MEM)
    control_b = lax.optimization_barrier(control.astype(jnp.bfloat16)).astype(jnp.float32)
    vertical = jnp.einsum('ab,bmc->amc', level_loc, control_b, precision=lax.Precision.HIGHEST)
    increment = smooth_columns(vertical)
    mixed = jnp.einsum('s,asmc->amc', extinction.astype(jnp.float32), members.astype(jnp.float32), precision=lax.Precision.HIGHEST)
    column_field = lax.optimization_barrier(jnp.sum(mixed * increment, axis=1)) * scale
    target = (owners[:, 0][:, None] * COL_DEV + pixel_columns).astype(jnp.int32)
    picked = jnp.take(column_field, target, axis=1)
    kernel_values = kernels.astype(jnp.float32)
    evolved = lax.optimization_barrier(jnp.sum(kernel_values * jnp.transpose(picked, (1, 0, 2)), axis=1))
    live_pixels = jnp.arange(BLK, dtype=jnp.int32)[None, :] < pixel_counts[:, None]
    misfit = jnp.where(live_pixels, obs_weight.astype(jnp.float32) * (evolved - innovation.astype(jnp.float32)), 0.0)
    contrib = kernel_values * misfit[:, None, :]
    flat_terms = jnp.transpose(contrib, (0, 2, 1)).reshape(-1, LEV)
    field_grad = jax.ops.segment_sum(flat_terms, target.reshape(-1), num_segments=NCOL).T
    member_grad = mixed * field_grad[:, None, :] * scale
    smoothed = smooth_columns(member_grad)
    smoothed_b = lax.optimization_barrier(smoothed.astype(jnp.bfloat16)).astype(jnp.float32)
    return control + jnp.einsum('ba,bmc->amc', level_loc, smoothed_b, precision=lax.Precision.HIGHEST)
```

```python
import functools
import math

import jax
import jax.numpy as jnp
import numpy as np
from jax import lax
from jax.experimental import pallas as pl
from jax.experimental.pallas import tpu as pltpu
from jax.sharding import PartitionSpec as P

LEV = 64
HALF = 4
LANES = 128
PAIR = 16
GROUP = 8
BF = jnp.bfloat16
F32 = jnp.float32


def level_matrix():
    index_levels = np.arange(LEV, dtype=np.float32)
    spread = np.float32(LEV / 8.0)
    distance = index_levels[:, None] - index_levels[None, :]
    matrix = np.exp(-distance * distance / (2 * spread * spread)) / (np.float32(2.5066283) * spread)
    return matrix.astype(BF)


def column_taps():
    offsets = np.arange(2 * HALF + 1, dtype=np.float32) - HALF
    spread = np.float32(HALF / 2.0)
    weights = np.exp(-offsets * offsets / (2 * spread * spread))
    return weights / np.sum(weights)


def tap_matrix(width):
    rows = np.arange(width + LANES)
    place = np.where(rows < width + HALF, rows, rows - width - 2 * HALF)
    gap = place[:, None] - np.arange(width)[None, :]
    near = (np.abs(gap) <= HALF) & (rows < width + 2 * HALF)[:, None]
    dense = np.where(near, column_taps()[np.clip(gap + HALF, 0, 2 * HALF)], 0.0).astype(np.float32)
    high = dense.astype(BF)
    low = (dense - high.astype(np.float32)).astype(BF)
    return jnp.asarray(high), jnp.asarray(low)


def spread_levels(matrix):
    dense = np.kron(matrix.astype(np.float32), np.eye(PAIR, dtype=np.float32))
    return jnp.asarray(dense.astype(BF))


def with_halo(value):
    count = lax.axis_size("horiz")
    length = value.shape[-1]
    up = [(i, i + 1) for i in range(count - 1)]
    down = [(j, i) for i, j in up]
    before = lax.ppermute(value[..., length - HALF :], "horiz", up)
    after = lax.ppermute(value[..., :HALF], "horiz", down)
    edges = jnp.concatenate([after, before], axis=-1)
    pad = [(0, 0)] * (value.ndim - 1) + [(0, LANES - 2 * HALF)]
    return jnp.concatenate([value, jnp.pad(edges, pad)], axis=-1)


def dot(a, b):
    return jnp.dot(a, b, preferred_element_type=F32)


def smooth_kernel(x_ref, hi_ref, lo_ref, out_ref):
    levels, members, ext = x_ref.shape
    x = x_ref[...].reshape(levels * members, ext)
    total = dot(x, hi_ref[...]) + dot(x, lo_ref[...])
    out_ref[...] = total.astype(BF).reshape(out_ref.shape)


def field_kernel(scale, all_ref, kron_ref, mixed_ref, out_ref):
    levels, members, width = mixed_ref.shape
    total = None
    for half in range(members // PAIR):
        part = pl.ds(half * PAIR, PAIR)
        x = all_ref[:, part, :].reshape(LEV * PAIR, width)
        inc = dot(kron_ref[...], x).reshape(levels, PAIR, width)
        term = jnp.sum(mixed_ref[:, part, :].astype(F32) * inc, axis=1)
        total = term if total is None else total + term
    total = total * scale
    for tile in range(width // LANES):
        out_ref[tile] = total[:, tile * LANES : (tile + 1) * LANES]


def forward_kernel(owner_ref, field_ref, kern_ref, col_ref, out_ref):
    blocks = col_ref.shape[0]
    tiles, levels = field_ref.shape[1], field_ref.shape[2]

    def step(group, carry):
        base = pl.multiple_of(group * GROUP, GROUP)
        cols = col_ref[pl.ds(base, GROUP), :]
        rows = []
        for i in range(GROUP):
            owner = owner_ref[base + i]
            col = jnp.broadcast_to(cols[i : i + 1, :], (levels, LANES))
            low = jnp.bitwise_and(col, LANES - 1)
            high = jnp.right_shift(col, 7)
            picked = jnp.take_along_axis(field_ref[owner, 0], low, axis=1)
            for tile in range(1, tiles):
                other = jnp.take_along_axis(field_ref[owner, tile], low, axis=1)
                picked = jnp.where(high == tile, other, picked)
            prod = picked * kern_ref[base + i].astype(F32)
            rows.append(jnp.sum(prod, axis=0, keepdims=True))
        out_ref[pl.ds(base, GROUP), :] = jnp.concatenate(rows, axis=0)
        return carry

    lax.fori_loop(0, blocks // GROUP, step, 0)


def adjoint_kernel(scale, owner_ref, kern_ref, col_ref, ev_ref, inn_ref, w_ref, out_ref):
    blocks = col_ref.shape[0]
    levels = kern_ref.shape[1]
    tiles = out_ref.shape[1] // levels
    out_ref[...] = jnp.zeros_like(out_ref)
    lane_row = lax.broadcasted_iota(jnp.int32, (LANES, LANES), 0)

    def step(group, carry):
        base = pl.multiple_of(group * GROUP, GROUP)
        cols = col_ref[pl.ds(base, GROUP), :]
        low = jnp.bitwise_and(cols, LANES - 1)
        high = jnp.right_shift(cols, 7)
        misfit = w_ref[pl.ds(base, GROUP), :] * (
            ev_ref[pl.ds(base, GROUP), :] - inn_ref[pl.ds(base, GROUP), :]
        )
        misfit = misfit * scale
        parts = [jnp.where(high == tile, misfit, 0.0) for tile in range(tiles)]
        for i in range(GROUP):
            owner = owner_ref[base + i]
            kern = kern_ref[base + i].astype(F32)
            left = jnp.concatenate(
                [(kern * part[i : i + 1, :]).astype(BF) for part in parts], axis=0
            )
            hot = jnp.where(lane_row == low[i : i + 1, :], 1.0, 0.0).astype(BF)
            out_ref[owner] += lax.dot_general(
                left, hot, (((1,), (1,)), ((), ())), preferred_element_type=F32
            )
        return carry

    lax.fori_loop(0, blocks // GROUP, step, 0)


def final_kernel(mixed_ref, fg_ref, kron_ref, hi_ref, lo_ref, control_ref, out_ref):
    levels, members, width = control_ref.shape
    ext = mixed_ref.shape[2]
    fg = fg_ref[...]
    for half in range(members // PAIR):
        part = pl.ds(half * PAIR, PAIR)
        grad = mixed_ref[:, part, :].astype(F32) * fg[:, None, :]
        grad = grad.reshape(LEV * PAIR, ext)
        high = grad.astype(BF)
        low = (grad - high.astype(F32)).astype(BF)
        mixed_levels = dot(kron_ref[...], high) + dot(kron_ref[...], low)
        high = mixed_levels.astype(BF)
        low = (mixed_levels - high.astype(F32)).astype(BF)
        total = dot(high, hi_ref[...]) + dot(high, lo_ref[...]) + dot(low, hi_ref[...])
        out_ref[:, part, :] = control_ref[:, part, :] + total.reshape(levels, PAIR, width)


def greet(partners):
    barrier = pltpu.get_barrier_semaphore()
    for device in partners:
        pl.semaphore_signal(barrier, inc=1, device_id=device, device_id_type=MESH)
    pl.semaphore_wait(barrier, len(partners))


def send(src, dst, send_sem, recv_sem, device):
    copy = pltpu.make_async_remote_copy(
        src_ref=src,
        dst_ref=dst,
        send_sem=send_sem,
        recv_sem=recv_sem,
        device_id=device,
        device_id_type=MESH,
    )
    copy.start()
    return copy


def others(axis, count):
    me = lax.axis_index(axis)
    return [lax.rem(me + k, count) for k in range(1, count)]


def gather_kernel(axis, count, x_ref, out_ref, send_sem, recv_sem):
    me = lax.axis_index(axis)
    peers = others(axis, count)
    greet([{axis: peer} for peer in peers])
    copies = [
        send(x_ref, out_ref.at[me], send_sem.at[k], recv_sem.at[k], {axis: peer})
        for k, peer in enumerate(peers)
    ]
    out_ref[me] = x_ref[...]
    for copy in copies:
        copy.wait()


def level_gather_kernel(x_ref, out_ref, far_s, far_r, near_s, near_r, on_s, on_r):
    me = lax.axis_index("lev")
    near = me + 1 - 2 * lax.rem(me, 2)
    far = lax.rem(me + 2, 4)
    greet([{"lev": near}, {"lev": far}])
    chunks = far_s.shape[0]
    rows = x_ref.shape[0] // chunks
    parts = [pl.ds(c * rows, rows) for c in range(chunks)]
    away = [
        send(x_ref.at[part], out_ref.at[me, part], far_s.at[c], far_r.at[c], {"lev": far})
        for c, part in enumerate(parts)
    ]
    beside = send(x_ref, out_ref.at[me], near_s, near_r, {"lev": near})
    out_ref[me] = x_ref[...]
    onward = []
    for c, part in enumerate(parts):
        away[c].wait_recv()
        block = out_ref.at[far, part]
        onward.append(send(block, block, on_s.at[c], on_r.at[c], {"lev": near}))
    for copy in away:
        copy.wait_send()
    beside.wait()
    for copy in onward:
        copy.wait()


def total_kernel(count, x_ref, out_ref, slots, send_a, recv_a, send_b, recv_b):
    me = lax.axis_index("lev")
    peers = others("lev", count)
    greet([{"lev": peer} for peer in peers])
    rows = x_ref.shape[0] // count
    copies = [
        send(
            x_ref.at[pl.ds(pl.multiple_of(peer * rows, rows), rows)],
            slots.at[k],
            send_a.at[k],
            recv_a.at[k],
            {"lev": peer},
        )
        for k, peer in enumerate(peers)
    ]
    mine = pl.ds(pl.multiple_of(me * rows, rows), rows)
    total = x_ref[mine, :]
    for k, copy in enumerate(copies):
        copy.wait()
        total = total + slots[k]
    out_ref[mine, :] = total
    block = out_ref.at[mine]
    copies = [
        send(block, block, send_b.at[k], recv_b.at[k], {"lev": peer})
        for k, peer in enumerate(peers)
    ]
    for copy in copies:
        copy.wait()


def return_kernel(count, levs, x_ref, out_ref, slots, send_a, recv_a, send_b, recv_b):
    me, lev = lax.axis_index("horiz"), lax.axis_index("lev")
    peers = others("horiz", count)
    sides = others("lev", levs)
    greet([{"horiz": peer} for peer in peers] + [{"lev": side} for side in sides])
    copies = [
        send(x_ref.at[peer], slots.at[k], send_a.at[k], recv_a.at[k], {"horiz": peer})
        for k, peer in enumerate(peers)
    ]
    total = x_ref[me]
    for k, copy in enumerate(copies):
        copy.wait()
        total = total + slots[k]
    out_ref[lev] = total
    block = out_ref.at[lev]
    copies = [
        send(block, block, send_b.at[k], recv_b.at[k], {"lev": side})
        for k, side in enumerate(sides)
    ]
    for copy in copies:
        copy.wait()


def vmem(count):
    return [pl.BlockSpec(memory_space=pltpu.VMEM)] * count


def smem(count):
    return [pl.BlockSpec(memory_space=pltpu.SMEM)] * count


MESH = pl.DeviceIdType.MESH
PARAMS = pltpu.CompilerParams(vmem_limit_bytes=48 * 1024 * 1024)


def call(kernel, shape, dtype, scalars, *args):
    return pl.pallas_call(
        kernel,
        out_shape=jax.ShapeDtypeStruct(shape, dtype),
        in_specs=smem(scalars) + vmem(len(args) - scalars),
        out_specs=pl.BlockSpec(memory_space=pltpu.VMEM),
        compiler_params=PARAMS,
    )(*args)


def exchange(kernel, number, shape, slots, sems, x):
    scratch = [pltpu.VMEM(slots, F32)] if slots else []
    scratch += [pltpu.SemaphoreType.DMA(size) for size in sems]
    return pl.pallas_call(
        kernel,
        out_shape=jax.ShapeDtypeStruct(shape, x.dtype),
        in_specs=vmem(1),
        out_specs=pl.BlockSpec(memory_space=pltpu.VMEM),
        scratch_shapes=scratch,
        compiler_params=pltpu.CompilerParams(
            vmem_limit_bytes=32 * 1024 * 1024, collective_id=number, has_side_effects=True
        ),
    )(x)


def body(
    control,
    members,
    extinction,
    kernels,
    innovation,
    obs_weight,
    owners,
    pixel_columns,
    pixel_counts,
):
    levels, mem_count, width = control.shape
    blocks, _, pixels = kernels.shape
    horiz = lax.axis_size("horiz")
    tiles = width // LANES
    level_loc = level_matrix()
    first = lax.axis_index("lev") * levels
    kron = lax.dynamic_slice_in_dim(
        spread_levels(level_loc), first * PAIR, levels * PAIR, 0
    )
    levs = lax.axis_size("lev")
    hi, lo = tap_matrix(width)
    scale = 1.0 / math.sqrt(mem_count)
    owner_ids = owners[:, 0]

    control_ext = with_halo(control.astype(BF))
    smooth = call(smooth_kernel, (levels, mem_count, width), BF, 0, control_ext, hi, lo)
    smooth_all = exchange(
        level_gather_kernel,
        0,
        (levs,) + smooth.shape,
        None,
        [(4,), (4,), (), (), (4,), (4,)],
        smooth,
    ).reshape((levs * levels,) + smooth.shape[1:])

    mixed = extinction[0] * members[:, 0].astype(F32)
    for species in range(1, members.shape[1]):
        mixed = mixed + extinction[species] * members[:, species].astype(F32)
    mixed_ext = with_halo(mixed.astype(BF))
    mixed_all = lax.all_gather(mixed_ext, "lev", axis=0, tiled=True)


    field = call(
        functools.partial(field_kernel, scale),
        (tiles, levels, LANES),
        F32,
        0,
        smooth_all,
        kron,
        mixed,
    )
    field_all = exchange(
        functools.partial(gather_kernel, "horiz", horiz),
        1,
        (horiz,) + field.shape,
        None,
        [(horiz - 1,)] * 2,
        field,
    )
    local = call(
        forward_kernel, (blocks, pixels), F32, 1, owner_ids, field_all, kernels, pixel_columns
    )
    evolved = exchange(
        functools.partial(total_kernel, levs),
        2,
        local.shape,
        (levs - 1, blocks // levs, pixels),
        [(levs - 1,)] * 4,
        local,
    )
    live = jnp.arange(pixels, dtype=jnp.int32)[None, :] < pixel_counts[:, None]
    weight = jnp.where(live, obs_weight.astype(F32), 0.0)
    partial = call(
        functools.partial(adjoint_kernel, scale),
        (horiz, tiles * levels, LANES),
        F32,
        1,
        owner_ids,
        kernels,
        pixel_columns,
        evolved,
        innovation.astype(F32),
        weight,
    )
    partial = partial.reshape(horiz, tiles, levels, LANES).transpose(0, 2, 1, 3)
    partial = partial.reshape(horiz, levels, width)
    edge = jnp.zeros((1, levels, HALF), F32)
    after = jnp.concatenate([partial[1:, :, :HALF], edge], axis=0)
    before = jnp.concatenate([edge, partial[:-1, :, width - HALF :]], axis=0)
    blank = jnp.zeros((horiz, levels, LANES - 2 * HALF), F32)
    partial = jnp.concatenate([partial, after, before, blank], axis=2)
    fg_all = exchange(
        functools.partial(return_kernel, horiz, levs),
        3,
        (levs, levels, width + LANES),
        (horiz - 1, levels, width + LANES),
        [(horiz - 1,)] * 2 + [(levs - 1,)] * 2,
        partial,
    ).reshape(levs * levels, width + LANES)
    return call(
        final_kernel, control.shape, F32, 0, mixed_all, fg_all, kron, hi, lo, control
    )


def solution(mesh):
    placed = (
        P("lev", None, "horiz"),
        P("lev", None, None, "horiz"),
        P(),
        P("horiz", "lev", None),
        P("horiz", None),
        P("horiz", None),
        P("horiz", None),
        P("horiz", None),
        P("horiz"),
    )
    return jax.shard_map(
        body, mesh=mesh, in_specs=placed, out_specs=P("lev", None, "horiz"), check_vma=False
    )
```

```python
import functools
import math

import jax
import jax.numpy as jnp
import numpy as np
from jax import lax
from jax.experimental import pallas as pl
from jax.experimental.pallas import tpu as pltpu
from jax.sharding import PartitionSpec as P

LEV = 64
HALF = 4
LANES = 128
PAIR = 16
GROUP = 8
BF = jnp.bfloat16
F32 = jnp.float32


def level_matrix():
    index_levels = np.arange(LEV, dtype=np.float32)
    spread = np.float32(LEV / 8.0)
    distance = index_levels[:, None] - index_levels[None, :]
    matrix = np.exp(-distance * distance / (2 * spread * spread)) / (np.float32(2.5066283) * spread)
    return matrix.astype(BF)


def column_taps():
    offsets = np.arange(2 * HALF + 1, dtype=np.float32) - HALF
    spread = np.float32(HALF / 2.0)
    weights = np.exp(-offsets * offsets / (2 * spread * spread))
    return weights / np.sum(weights)


def tap_matrix(width):
    rows = np.arange(width + LANES)
    place = np.where(rows < width + HALF, rows, rows - width - 2 * HALF)
    gap = place[:, None] - np.arange(width)[None, :]
    near = (np.abs(gap) <= HALF) & (rows < width + 2 * HALF)[:, None]
    dense = np.where(near, column_taps()[np.clip(gap + HALF, 0, 2 * HALF)], 0.0).astype(np.float32)
    high = dense.astype(BF)
    low = (dense - high.astype(np.float32)).astype(BF)
    return jnp.asarray(high), jnp.asarray(low)


def spread_levels(matrix):
    dense = np.kron(matrix.astype(np.float32), np.eye(PAIR, dtype=np.float32))
    return jnp.asarray(dense.astype(BF))


def dot(a, b):
    return jnp.dot(a, b, preferred_element_type=F32)


def field_kernel(scale, all_ref, kron_ref, mixed_ref, out_ref):
    levels, members, width = mixed_ref.shape
    total = None
    for half in range(members // PAIR):
        part = pl.ds(half * PAIR, PAIR)
        x = all_ref[:, part, :].reshape(LEV * PAIR, width)
        inc = dot(kron_ref[...], x).reshape(levels, PAIR, width)
        term = jnp.sum(mixed_ref[:, part, :].astype(F32) * inc, axis=1)
        total = term if total is None else total + term
    total = total * scale
    for tile in range(width // LANES):
        out_ref[tile] = total[:, tile * LANES : (tile + 1) * LANES]


def forward_kernel(owner_ref, field_ref, kern_ref, col_ref, out_ref):
    blocks = col_ref.shape[0]
    tiles, levels = field_ref.shape[1], field_ref.shape[2]

    def step(group, carry):
        base = pl.multiple_of(group * GROUP, GROUP)
        cols = col_ref[pl.ds(base, GROUP), :]
        rows = []
        for i in range(GROUP):
            owner = owner_ref[base + i]
            col = jnp.broadcast_to(cols[i : i + 1, :], (levels, LANES))
            low = jnp.bitwise_and(col, LANES - 1)
            high = jnp.right_shift(col, 7)
            picked = jnp.take_along_axis(field_ref[owner, 0], low, axis=1)
            for tile in range(1, tiles):
                other = jnp.take_along_axis(field_ref[owner, tile], low, axis=1)
                picked = jnp.where(high == tile, other, picked)
            prod = picked * kern_ref[base + i].astype(F32)
            rows.append(jnp.sum(prod, axis=0, keepdims=True))
        out_ref[pl.ds(base, GROUP), :] = jnp.concatenate(rows, axis=0)
        return carry

    lax.fori_loop(0, blocks // GROUP, step, 0)


def adjoint_kernel(scale, owner_ref, kern_ref, col_ref, ev_ref, inn_ref, w_ref, out_ref):
    blocks = col_ref.shape[0]
    levels = kern_ref.shape[1]
    tiles = out_ref.shape[1] // levels
    out_ref[...] = jnp.zeros_like(out_ref)
    lane_row = lax.broadcasted_iota(jnp.int32, (LANES, LANES), 0).astype(F32).astype(BF)
    one, zero = jnp.ones((), BF), jnp.zeros((), BF)

    def step(group, carry):
        base = pl.multiple_of(group * GROUP, GROUP)
        cols = col_ref[pl.ds(base, GROUP), :]
        low = jnp.bitwise_and(cols, LANES - 1).astype(F32)
        high = jnp.right_shift(cols, 7)
        misfit = w_ref[pl.ds(base, GROUP), :] * (
            ev_ref[pl.ds(base, GROUP), :] - inn_ref[pl.ds(base, GROUP), :]
        )
        misfit = misfit * scale
        parts = [jnp.where(high == tile, misfit, 0.0) for tile in range(tiles)]
        for i in range(GROUP):
            owner = owner_ref[base + i]
            kern = kern_ref[base + i].astype(F32)
            left = jnp.concatenate(
                [(kern * part[i : i + 1, :]).astype(BF) for part in parts], axis=0
            )
            row = jnp.broadcast_to(low[i : i + 1, :], (LANES, LANES)).astype(BF)
            hot = jnp.where(lane_row == row, one, zero)
            out_ref[owner] += lax.dot_general(
                left, hot, (((1,), (1,)), ((), ())), preferred_element_type=F32
            )
        return carry

    lax.fori_loop(0, blocks // GROUP, step, 0)


def final_kernel(mixed_ref, fg_ref, kron_ref, hi_ref, lo_ref, control_ref, out_ref):
    levels, members, width = control_ref.shape
    ext = mixed_ref.shape[2]
    fg = fg_ref[...]
    for half in range(members // PAIR):
        part = pl.ds(half * PAIR, PAIR)
        grad = mixed_ref[:, part, :].astype(F32) * fg[:, None, :]
        grad = grad.reshape(LEV * PAIR, ext)
        high = grad.astype(BF)
        low = (grad - high.astype(F32)).astype(BF)
        mixed_levels = dot(kron_ref[...], high) + dot(kron_ref[...], low)
        high = mixed_levels.astype(BF)
        low = (mixed_levels - high.astype(F32)).astype(BF)
        total = dot(high, hi_ref[...]) + dot(high, lo_ref[...]) + dot(low, hi_ref[...])
        out_ref[:, part, :] = control_ref[:, part, :] + total.reshape(levels, PAIR, width)


def greet(partners):
    barrier = pltpu.get_barrier_semaphore()
    for device in partners:
        pl.semaphore_signal(barrier, inc=1, device_id=device, device_id_type=MESH)
    pl.semaphore_wait(barrier, len(partners))


def send(src, dst, send_sem, recv_sem, device):
    copy = pltpu.make_async_remote_copy(
        src_ref=src,
        dst_ref=dst,
        send_sem=send_sem,
        recv_sem=recv_sem,
        device_id=device,
        device_id_type=MESH,
    )
    copy.start()
    return copy


def others(axis, count):
    me = lax.axis_index(axis)
    return [lax.rem(me + k, count) for k in range(1, count)]


def prepare_kernel(
    count,
    ext_ref,
    control_ref,
    members_ref,
    hi_ref,
    lo_ref,
    mixed_ref,
    ext_out,
    smooth_ref,
    out_tiles,
    in_tiles,
    send_sem,
    recv_sem,
):
    levels, members, width = control_ref.shape
    me = lax.axis_index("horiz")
    right, left = lax.rem(me + 1, count), lax.rem(me + count - 1, count)
    greet([{"horiz": right}, {"horiz": left}])
    lane = lax.broadcasted_iota(jnp.int32, (levels * members, LANES), 1)

    def mix(tile):
        part = pl.ds(tile * LANES, LANES)
        total = ext_ref[0] * members_ref[:, 0, :, part].astype(F32)
        for species in range(1, members_ref.shape[1]):
            total = total + ext_ref[species] * members_ref[:, species, :, part].astype(F32)
        mixed_ref[:, :, part] = total
        ext_out[:, :, part] = total.astype(BF)
        return total.reshape(levels * members, LANES)

    def own(tile):
        return control_ref[:, :, pl.ds(tile * LANES, LANES)].reshape(levels * members, LANES)

    last = width // LANES - 1
    first_mix, last_mix = mix(0), mix(last)
    to_left = jnp.where(lane < HALF, own(0), pltpu.roll(first_mix, 8, 1))
    to_right = jnp.where(lane < 8, pltpu.roll(own(last), 8, 1), pltpu.roll(last_mix, 16, 1))
    out_tiles[0] = to_left.astype(BF)
    out_tiles[1] = to_right.astype(BF)
    copies = [
        send(out_tiles.at[k], in_tiles.at[k], send_sem.at[k], recv_sem.at[k], {"horiz": peer})
        for k, peer in enumerate((left, right))
    ]
    for tile in range(1, last):
        mix(tile)
    x = control_ref[...].astype(BF).reshape(levels * members, width)
    total = dot(x, hi_ref[pl.ds(0, width), :]) + dot(x, lo_ref[pl.ds(0, width), :])
    for copy in copies:
        copy.wait()
    after = HALF * jnp.where(me < count - 1, 1, 0)
    before = HALF * jnp.where(me > 0, 1, 0)
    bit = jnp.bitwise_and(lane, 7)
    halo = jnp.where(bit < after, in_tiles[0].astype(F32), 0.0)
    halo = jnp.where(
        (bit >= HALF) & (bit < HALF + before), in_tiles[1].astype(F32), halo
    )
    shifted = jnp.where(lane < 8, pltpu.roll(halo, LANES - 8, 1), 0.0)
    ext_out[:, :, pl.ds(width, LANES)] = shifted.astype(BF).reshape(levels, members, LANES)
    halo = jnp.where(lane < 8, halo, 0.0).astype(BF)
    total = total + dot(halo, hi_ref[pl.ds(width, LANES), :])
    total = total + dot(halo, lo_ref[pl.ds(width, LANES), :])
    smooth_ref[...] = total.astype(BF).reshape(levels, members, width)


def gather_kernel(axis, count, x_ref, out_ref, send_sem, recv_sem):
    me = lax.axis_index(axis)
    peers = others(axis, count)
    greet([{axis: peer} for peer in peers])
    copies = [
        send(x_ref, out_ref.at[me], send_sem.at[k], recv_sem.at[k], {axis: peer})
        for k, peer in enumerate(peers)
    ]
    out_ref[me] = x_ref[...]
    for copy in copies:
        copy.wait()


def level_gather_kernel(x_ref, out_ref, far_s, far_r, near_s, near_r, on_s, on_r):
    me = lax.axis_index("lev")
    near = me + 1 - 2 * lax.rem(me, 2)
    far = lax.rem(me + 2, 4)
    greet([{"lev": near}, {"lev": far}])
    chunks = far_s.shape[0]
    rows = x_ref.shape[0] // chunks
    parts = [pl.ds(c * rows, rows) for c in range(chunks)]
    away = [
        send(x_ref.at[part], out_ref.at[me, part], far_s.at[c], far_r.at[c], {"lev": far})
        for c, part in enumerate(parts)
    ]
    beside = send(x_ref, out_ref.at[me], near_s, near_r, {"lev": near})
    out_ref[me] = x_ref[...]
    onward = []
    for c, part in enumerate(parts):
        away[c].wait_recv()
        block = out_ref.at[far, part]
        onward.append(send(block, block, on_s.at[c], on_r.at[c], {"lev": near}))
    for copy in away:
        copy.wait_send()
    beside.wait()
    for copy in onward:
        copy.wait()


def total_kernel(count, x_ref, out_ref, slots, send_a, recv_a, send_b, recv_b):
    me = lax.axis_index("lev")
    peers = others("lev", count)
    greet([{"lev": peer} for peer in peers])
    rows = x_ref.shape[0] // count
    copies = [
        send(
            x_ref.at[pl.ds(pl.multiple_of(peer * rows, rows), rows)],
            slots.at[k],
            send_a.at[k],
            recv_a.at[k],
            {"lev": peer},
        )
        for k, peer in enumerate(peers)
    ]
    mine = pl.ds(pl.multiple_of(me * rows, rows), rows)
    total = x_ref[mine, :]
    for k, copy in enumerate(copies):
        copy.wait()
        total = total + slots[k]
    out_ref[mine, :] = total
    block = out_ref.at[mine]
    copies = [
        send(block, block, send_b.at[k], recv_b.at[k], {"lev": peer})
        for k, peer in enumerate(peers)
    ]
    for copy in copies:
        copy.wait()


def return_kernel(count, levs, x_ref, out_ref, slots, send_a, recv_a, send_b, recv_b):
    me, lev = lax.axis_index("horiz"), lax.axis_index("lev")
    peers = others("horiz", count)
    sides = others("lev", levs)
    greet([{"horiz": peer} for peer in peers] + [{"lev": side} for side in sides])
    copies = [
        send(x_ref.at[peer], slots.at[k], send_a.at[k], recv_a.at[k], {"horiz": peer})
        for k, peer in enumerate(peers)
    ]
    total = x_ref[me]
    for k, copy in enumerate(copies):
        copy.wait()
        total = total + slots[k]
    out_ref[lev] = total
    block = out_ref.at[lev]
    copies = [
        send(block, block, send_b.at[k], recv_b.at[k], {"lev": side})
        for k, side in enumerate(sides)
    ]
    for copy in copies:
        copy.wait()


def vmem(count):
    return [pl.BlockSpec(memory_space=pltpu.VMEM)] * count


def smem(count):
    return [pl.BlockSpec(memory_space=pltpu.SMEM)] * count


MESH = pl.DeviceIdType.MESH
PARAMS = pltpu.CompilerParams(vmem_limit_bytes=48 * 1024 * 1024)


def call(kernel, shape, dtype, scalars, *args):
    return pl.pallas_call(
        kernel,
        out_shape=jax.ShapeDtypeStruct(shape, dtype),
        in_specs=smem(scalars) + vmem(len(args) - scalars),
        out_specs=pl.BlockSpec(memory_space=pltpu.VMEM),
        compiler_params=PARAMS,
    )(*args)


def exchange(kernel, number, shape, slots, sems, x):
    scratch = [pltpu.VMEM(slots, F32)] if slots else []
    scratch += [pltpu.SemaphoreType.DMA(size) for size in sems]
    return pl.pallas_call(
        kernel,
        out_shape=jax.ShapeDtypeStruct(shape, x.dtype),
        in_specs=vmem(1),
        out_specs=pl.BlockSpec(memory_space=pltpu.VMEM),
        scratch_shapes=scratch,
        compiler_params=pltpu.CompilerParams(
            vmem_limit_bytes=32 * 1024 * 1024, collective_id=number, has_side_effects=True
        ),
    )(x)


def body(
    control,
    members,
    extinction,
    kernels,
    innovation,
    obs_weight,
    owners,
    pixel_columns,
    pixel_counts,
):
    levels, mem_count, width = control.shape
    blocks, _, pixels = kernels.shape
    horiz = lax.axis_size("horiz")
    tiles = width // LANES
    level_loc = level_matrix()
    first = lax.axis_index("lev") * levels
    kron = lax.dynamic_slice_in_dim(
        spread_levels(level_loc), first * PAIR, levels * PAIR, 0
    )
    levs = lax.axis_size("lev")
    hi, lo = tap_matrix(width)
    scale = 1.0 / math.sqrt(mem_count)
    owner_ids = owners[:, 0]

    strip = (levels, mem_count, width)
    edge_tiles = pltpu.VMEM((2, levels * mem_count, LANES), BF)
    mixed, mixed_ext, smooth = pl.pallas_call(
        functools.partial(prepare_kernel, horiz),
        out_shape=[
            jax.ShapeDtypeStruct(strip, F32),
            jax.ShapeDtypeStruct((levels, mem_count, width + LANES), BF),
            jax.ShapeDtypeStruct(strip, BF),
        ],
        in_specs=smem(1) + vmem(4),
        out_specs=vmem(3),
        scratch_shapes=[edge_tiles, edge_tiles] + [pltpu.SemaphoreType.DMA((2,))] * 2,
        compiler_params=pltpu.CompilerParams(
            vmem_limit_bytes=40 * 1024 * 1024, collective_id=4, has_side_effects=True
        ),
    )(extinction, control, members, hi, lo)
    smooth_all = exchange(
        level_gather_kernel,
        0,
        (levs,) + smooth.shape,
        None,
        [(4,), (4,), (), (), (4,), (4,)],
        smooth,
    ).reshape((levs * levels,) + smooth.shape[1:])

    smooth_all, mixed_ext = lax.optimization_barrier((smooth_all, mixed_ext))
    mixed_all = lax.all_gather(mixed_ext, "lev", axis=0, tiled=True)

    field = call(
        functools.partial(field_kernel, scale),
        (tiles, levels, LANES),
        F32,
        0,
        smooth_all,
        kron,
        mixed,
    )
    field_all = exchange(
        functools.partial(gather_kernel, "horiz", horiz),
        1,
        (horiz,) + field.shape,
        None,
        [(horiz - 1,)] * 2,
        field,
    )
    local = call(
        forward_kernel, (blocks, pixels), F32, 1, owner_ids, field_all, kernels, pixel_columns
    )
    evolved = exchange(
        functools.partial(total_kernel, levs),
        2,
        local.shape,
        (levs - 1, blocks // levs, pixels),
        [(levs - 1,)] * 4,
        local,
    )
    live = jnp.arange(pixels, dtype=jnp.int32)[None, :] < pixel_counts[:, None]
    weight = jnp.where(live, obs_weight.astype(F32), 0.0)
    partial = call(
        functools.partial(adjoint_kernel, scale),
        (horiz, tiles * levels, LANES),
        F32,
        1,
        owner_ids,
        kernels,
        pixel_columns,
        evolved,
        innovation.astype(F32),
        weight,
    )
    partial = partial.reshape(horiz, tiles, levels, LANES).transpose(0, 2, 1, 3)
    partial = partial.reshape(horiz, levels, width)
    edge = jnp.zeros((1, levels, HALF), F32)
    after = jnp.concatenate([partial[1:, :, :HALF], edge], axis=0)
    before = jnp.concatenate([edge, partial[:-1, :, width - HALF :]], axis=0)
    blank = jnp.zeros((horiz, levels, LANES - 2 * HALF), F32)
    partial = jnp.concatenate([partial, after, before, blank], axis=2)
    fg_all = exchange(
        functools.partial(return_kernel, horiz, levs),
        3,
        (levs, levels, width + LANES),
        (horiz - 1, levels, width + LANES),
        [(horiz - 1,)] * 2 + [(levs - 1,)] * 2,
        partial,
    ).reshape(levs * levels, width + LANES)
    return call(
        final_kernel, control.shape, F32, 0, mixed_all, fg_all, kron, hi, lo, control
    )


def solution(mesh):
    placed = (
        P("lev", None, "horiz"),
        P("lev", None, None, "horiz"),
        P(),
        P("horiz", "lev", None),
        P("horiz", None),
        P("horiz", None),
        P("horiz", None),
        P("horiz", None),
        P("horiz"),
    )
    return jax.shard_map(
        body, mesh=mesh, in_specs=placed, out_specs=P("lev", None, "horiz"), check_vma=False
    )
```

```python
import functools
import math

import jax
import jax.numpy as jnp
import numpy as np
from jax import lax
from jax.experimental import pallas as pl
from jax.experimental.pallas import tpu as pltpu
from jax.sharding import PartitionSpec as P

LEV = 64
HALF = 4
LANES = 128
PAIR = 16
GROUP = 32
BF = jnp.bfloat16
F32 = jnp.float32


def level_matrix():
    index_levels = np.arange(LEV, dtype=np.float32)
    spread = np.float32(LEV / 8.0)
    distance = index_levels[:, None] - index_levels[None, :]
    matrix = np.exp(-distance * distance / (2 * spread * spread)) / (np.float32(2.5066283) * spread)
    return matrix.astype(BF)


def column_taps():
    offsets = np.arange(2 * HALF + 1, dtype=np.float32) - HALF
    spread = np.float32(HALF / 2.0)
    weights = np.exp(-offsets * offsets / (2 * spread * spread))
    return weights / np.sum(weights)


def tap_matrix(width):
    rows = np.arange(width + LANES)
    place = np.where(rows < width + HALF, rows, rows - width - 2 * HALF)
    gap = place[:, None] - np.arange(width)[None, :]
    near = (np.abs(gap) <= HALF) & (rows < width + 2 * HALF)[:, None]
    dense = np.where(near, column_taps()[np.clip(gap + HALF, 0, 2 * HALF)], 0.0).astype(np.float32)
    high = dense.astype(BF)
    low = (dense - high.astype(np.float32)).astype(BF)
    return jnp.asarray(high), jnp.asarray(low)


def spread_levels(matrix):
    dense = np.kron(matrix.astype(np.float32), np.eye(PAIR, dtype=np.float32))
    return jnp.asarray(dense.astype(BF))


def dot(a, b):
    return jnp.dot(a, b, preferred_element_type=F32)


def field_kernel(scale, all_ref, kron_ref, mixed_ref, out_ref):
    levels, members, width = mixed_ref.shape
    total = None
    for half in range(members // PAIR):
        part = pl.ds(half * PAIR, PAIR)
        x = all_ref[:, part, :].reshape(LEV * PAIR, width)
        inc = dot(kron_ref[...], x).reshape(levels, PAIR, width)
        term = jnp.sum(mixed_ref[:, part, :].astype(F32) * inc, axis=1)
        total = term if total is None else total + term
    total = total * scale
    for tile in range(width // LANES):
        out_ref[tile] = total[:, tile * LANES : (tile + 1) * LANES]


def forward_kernel(owner_ref, field_ref, kern_ref, col_ref, out_ref):
    blocks = col_ref.shape[0]
    tiles, levels = field_ref.shape[1], field_ref.shape[2]

    def step(group, carry):
        base = pl.multiple_of(group * GROUP, GROUP)
        cols = col_ref[pl.ds(base, GROUP), :]
        rows = []
        for i in range(GROUP):
            owner = owner_ref[base + i]
            col = jnp.broadcast_to(cols[i : i + 1, :], (levels, LANES))
            low = jnp.bitwise_and(col, LANES - 1)
            high = jnp.right_shift(col, 7)
            picked = jnp.take_along_axis(field_ref[owner, 0], low, axis=1)
            for tile in range(1, tiles):
                other = jnp.take_along_axis(field_ref[owner, tile], low, axis=1)
                picked = jnp.where(high == tile, other, picked)
            prod = picked * kern_ref[base + i].astype(F32)
            rows.append(jnp.sum(prod, axis=0, keepdims=True))
        out_ref[pl.ds(base, GROUP), :] = jnp.concatenate(rows, axis=0)
        return carry

    lax.fori_loop(0, blocks // GROUP, step, 0)


def adjoint_kernel(scale, owner_ref, kern_ref, col_ref, ev_ref, inn_ref, w_ref, out_ref):
    blocks = col_ref.shape[0]
    levels = kern_ref.shape[1]
    tiles = out_ref.shape[2] // levels
    out_ref[...] = jnp.zeros_like(out_ref)
    lane_row = lax.broadcasted_iota(jnp.int32, (LANES, LANES), 0).astype(F32).astype(BF)
    one, zero = jnp.ones((), BF), jnp.zeros((), BF)

    def step(group, carry):
        base = pl.multiple_of(group * GROUP, GROUP)
        cols = col_ref[pl.ds(base, GROUP), :]
        low = jnp.bitwise_and(cols, LANES - 1).astype(F32)
        high = jnp.right_shift(cols, 7)
        misfit = w_ref[pl.ds(base, GROUP), :] * (
            ev_ref[pl.ds(base, GROUP), :] - inn_ref[pl.ds(base, GROUP), :]
        )
        misfit = misfit * scale
        parts = [jnp.where(high == tile, misfit, 0.0) for tile in range(tiles)]
        for i in range(GROUP):
            owner = owner_ref[base + i]
            kern = kern_ref[base + i].astype(F32)
            rows = jnp.concatenate(
                [(kern * part[i : i + 1, :]).astype(BF) for part in parts], axis=0
            )
            row = jnp.broadcast_to(low[i : i + 1, :], (LANES, LANES)).astype(BF)
            hot = jnp.where(lane_row == row, one, zero)
            out_ref[owner] += lax.dot_general(
                hot, rows, (((1,), (1,)), ((), ())), preferred_element_type=F32
            )
        return carry

    lax.fori_loop(0, blocks // GROUP, step, 0)


def final_kernel(mixed_ref, fg_ref, kron_ref, hi_ref, lo_ref, control_ref, out_ref):
    levels, members, width = control_ref.shape
    ext = mixed_ref.shape[2]
    fg = fg_ref[...]
    for half in range(members // PAIR):
        part = pl.ds(half * PAIR, PAIR)
        grad = mixed_ref[:, part, :].astype(F32) * fg[:, None, :]
        grad = grad.reshape(LEV * PAIR, ext)
        high = grad.astype(BF)
        low = (grad - high.astype(F32)).astype(BF)
        mixed_levels = dot(kron_ref[...], high) + dot(kron_ref[...], low)
        high = mixed_levels.astype(BF)
        low = (mixed_levels - high.astype(F32)).astype(BF)
        total = dot(high, hi_ref[...]) + dot(high, lo_ref[...]) + dot(low, hi_ref[...])
        out_ref[:, part, :] = control_ref[:, part, :] + total.reshape(levels, PAIR, width)


def greet(partners):
    barrier = pltpu.get_barrier_semaphore()
    for device in partners:
        pl.semaphore_signal(barrier, inc=1, device_id=device, device_id_type=MESH)
    pl.semaphore_wait(barrier, len(partners))


def send(src, dst, send_sem, recv_sem, device):
    copy = pltpu.make_async_remote_copy(
        src_ref=src,
        dst_ref=dst,
        send_sem=send_sem,
        recv_sem=recv_sem,
        device_id=device,
        device_id_type=MESH,
    )
    copy.start()
    return copy


def others(axis, count):
    me = lax.axis_index(axis)
    return [lax.rem(me + k, count) for k in range(1, count)]


def prepare_kernel(
    count,
    ext_ref,
    control_ref,
    members_ref,
    hi_ref,
    lo_ref,
    mixed_ref,
    ext_out,
    smooth_ref,
    out_tiles,
    in_tiles,
    send_sem,
    recv_sem,
):
    levels, members, width = control_ref.shape
    me = lax.axis_index("horiz")
    right, left = lax.rem(me + 1, count), lax.rem(me + count - 1, count)
    greet([{"horiz": right}, {"horiz": left}])
    lane = lax.broadcasted_iota(jnp.int32, (levels * members, LANES), 1)

    def mix(tile):
        part = pl.ds(tile * LANES, LANES)
        total = ext_ref[0] * members_ref[:, 0, :, part].astype(F32)
        for species in range(1, members_ref.shape[1]):
            total = total + ext_ref[species] * members_ref[:, species, :, part].astype(F32)
        mixed_ref[:, :, part] = total
        ext_out[:, :, part] = total.astype(BF)
        return total.reshape(levels * members, LANES)

    def own(tile):
        return control_ref[:, :, pl.ds(tile * LANES, LANES)].reshape(levels * members, LANES)

    last = width // LANES - 1
    first_mix, last_mix = mix(0), mix(last)
    to_left = jnp.where(lane < HALF, own(0), pltpu.roll(first_mix, 8, 1))
    to_right = jnp.where(lane < 8, pltpu.roll(own(last), 8, 1), pltpu.roll(last_mix, 16, 1))
    out_tiles[0] = to_left.astype(BF)
    out_tiles[1] = to_right.astype(BF)
    copies = [
        send(out_tiles.at[k], in_tiles.at[k], send_sem.at[k], recv_sem.at[k], {"horiz": peer})
        for k, peer in enumerate((left, right))
    ]
    for tile in range(1, last):
        mix(tile)
    x = control_ref[...].astype(BF).reshape(levels * members, width)
    total = dot(x, hi_ref[pl.ds(0, width), :]) + dot(x, lo_ref[pl.ds(0, width), :])
    for copy in copies:
        copy.wait()
    after = HALF * jnp.where(me < count - 1, 1, 0)
    before = HALF * jnp.where(me > 0, 1, 0)
    bit = jnp.bitwise_and(lane, 7)
    halo = jnp.where(bit < after, in_tiles[0].astype(F32), 0.0)
    halo = jnp.where(
        (bit >= HALF) & (bit < HALF + before), in_tiles[1].astype(F32), halo
    )
    shifted = jnp.where(lane < 8, pltpu.roll(halo, LANES - 8, 1), 0.0)
    ext_out[:, :, pl.ds(width, LANES)] = shifted.astype(BF).reshape(levels, members, LANES)
    halo = jnp.where(lane < 8, halo, 0.0).astype(BF)
    total = total + dot(halo, hi_ref[pl.ds(width, LANES), :])
    total = total + dot(halo, lo_ref[pl.ds(width, LANES), :])
    smooth_ref[...] = total.astype(BF).reshape(levels, members, width)


def gather_kernel(axis, count, x_ref, out_ref, send_sem, recv_sem):
    me = lax.axis_index(axis)
    peers = others(axis, count)
    greet([{axis: peer} for peer in peers])
    copies = [
        send(x_ref, out_ref.at[me], send_sem.at[k], recv_sem.at[k], {axis: peer})
        for k, peer in enumerate(peers)
    ]
    out_ref[me] = x_ref[...]
    for copy in copies:
        copy.wait()


def level_gather_kernel(x_ref, out_ref, far_s, far_r, near_s, near_r, on_s, on_r):
    me = lax.axis_index("lev")
    near = me + 1 - 2 * lax.rem(me, 2)
    far = lax.rem(me + 2, 4)
    greet([{"lev": near}, {"lev": far}])
    chunks = far_s.shape[0]
    rows = x_ref.shape[0] // chunks
    parts = [pl.ds(c * rows, rows) for c in range(chunks)]
    away = [
        send(x_ref.at[part], out_ref.at[me, part], far_s.at[c], far_r.at[c], {"lev": far})
        for c, part in enumerate(parts)
    ]
    beside = send(x_ref, out_ref.at[me], near_s, near_r, {"lev": near})
    out_ref[me] = x_ref[...]
    onward = []
    for c, part in enumerate(parts):
        away[c].wait_recv()
        block = out_ref.at[far, part]
        onward.append(send(block, block, on_s.at[c], on_r.at[c], {"lev": near}))
    for copy in away:
        copy.wait_send()
    beside.wait()
    for copy in onward:
        copy.wait()


def total_kernel(count, x_ref, out_ref, slots, send_a, recv_a, send_b, recv_b):
    me = lax.axis_index("lev")
    peers = others("lev", count)
    greet([{"lev": peer} for peer in peers])
    rows = x_ref.shape[0] // count
    copies = [
        send(
            x_ref.at[pl.ds(pl.multiple_of(peer * rows, rows), rows)],
            slots.at[k],
            send_a.at[k],
            recv_a.at[k],
            {"lev": peer},
        )
        for k, peer in enumerate(peers)
    ]
    mine = pl.ds(pl.multiple_of(me * rows, rows), rows)
    total = x_ref[mine, :]
    for k, copy in enumerate(copies):
        copy.wait()
        total = total + slots[k]
    out_ref[mine, :] = total
    block = out_ref.at[mine]
    copies = [
        send(block, block, send_b.at[k], recv_b.at[k], {"lev": peer})
        for k, peer in enumerate(peers)
    ]
    for copy in copies:
        copy.wait()


def return_kernel(count, levs, x_ref, out_ref, slots, send_a, recv_a, send_b, recv_b):
    me, lev = lax.axis_index("horiz"), lax.axis_index("lev")
    peers = others("horiz", count)
    sides = others("lev", levs)
    greet([{"horiz": peer} for peer in peers] + [{"lev": side} for side in sides])
    copies = [
        send(x_ref.at[peer], slots.at[k], send_a.at[k], recv_a.at[k], {"horiz": peer})
        for k, peer in enumerate(peers)
    ]
    total = x_ref[me]
    for k, copy in enumerate(copies):
        copy.wait()
        total = total + slots[k]
    out_ref[lev] = total
    block = out_ref.at[lev]
    copies = [
        send(block, block, send_b.at[k], recv_b.at[k], {"lev": side})
        for k, side in enumerate(sides)
    ]
    for copy in copies:
        copy.wait()


def vmem(count):
    return [pl.BlockSpec(memory_space=pltpu.VMEM)] * count


def smem(count):
    return [pl.BlockSpec(memory_space=pltpu.SMEM)] * count


MESH = pl.DeviceIdType.MESH
PARAMS = pltpu.CompilerParams(vmem_limit_bytes=48 * 1024 * 1024)


def call(kernel, shape, dtype, scalars, *args):
    return pl.pallas_call(
        kernel,
        out_shape=jax.ShapeDtypeStruct(shape, dtype),
        in_specs=smem(scalars) + vmem(len(args) - scalars),
        out_specs=pl.BlockSpec(memory_space=pltpu.VMEM),
        compiler_params=PARAMS,
    )(*args)


def exchange(kernel, number, shape, slots, sems, x):
    scratch = [pltpu.VMEM(slots, F32)] if slots else []
    scratch += [pltpu.SemaphoreType.DMA(size) for size in sems]
    return pl.pallas_call(
        kernel,
        out_shape=jax.ShapeDtypeStruct(shape, x.dtype),
        in_specs=vmem(1),
        out_specs=pl.BlockSpec(memory_space=pltpu.VMEM),
        scratch_shapes=scratch,
        compiler_params=pltpu.CompilerParams(
            vmem_limit_bytes=32 * 1024 * 1024, collective_id=number, has_side_effects=True
        ),
    )(x)


def body(
    control,
    members,
    extinction,
    kernels,
    innovation,
    obs_weight,
    owners,
    pixel_columns,
    pixel_counts,
):
    levels, mem_count, width = control.shape
    blocks, _, pixels = kernels.shape
    horiz = lax.axis_size("horiz")
    tiles = width // LANES
    level_loc = level_matrix()
    first = lax.axis_index("lev") * levels
    kron = lax.dynamic_slice_in_dim(
        spread_levels(level_loc), first * PAIR, levels * PAIR, 0
    )
    levs = lax.axis_size("lev")
    hi, lo = tap_matrix(width)
    scale = 1.0 / math.sqrt(mem_count)
    owner_ids = owners[:, 0]

    strip = (levels, mem_count, width)
    edge_tiles = pltpu.VMEM((2, levels * mem_count, LANES), BF)
    mixed, mixed_ext, smooth = pl.pallas_call(
        functools.partial(prepare_kernel, horiz),
        out_shape=[
            jax.ShapeDtypeStruct(strip, F32),
            jax.ShapeDtypeStruct((levels, mem_count, width + LANES), BF),
            jax.ShapeDtypeStruct(strip, BF),
        ],
        in_specs=smem(1) + vmem(4),
        out_specs=vmem(3),
        scratch_shapes=[edge_tiles, edge_tiles] + [pltpu.SemaphoreType.DMA((2,))] * 2,
        compiler_params=pltpu.CompilerParams(
            vmem_limit_bytes=40 * 1024 * 1024, collective_id=4, has_side_effects=True
        ),
    )(extinction, control, members, hi, lo)
    smooth_all = exchange(
        level_gather_kernel,
        0,
        (levs,) + smooth.shape,
        None,
        [(4,), (4,), (), (), (4,), (4,)],
        smooth,
    ).reshape((levs * levels,) + smooth.shape[1:])

    smooth_all, mixed_ext = lax.optimization_barrier((smooth_all, mixed_ext))
    mixed_all = lax.all_gather(mixed_ext, "lev", axis=0, tiled=True)

    field = call(
        functools.partial(field_kernel, scale),
        (tiles, levels, LANES),
        F32,
        0,
        smooth_all,
        kron,
        mixed,
    )
    field_all = exchange(
        functools.partial(gather_kernel, "horiz", horiz),
        1,
        (horiz,) + field.shape,
        None,
        [(horiz - 1,)] * 2,
        field,
    )
    local = call(
        forward_kernel, (blocks, pixels), F32, 1, owner_ids, field_all, kernels, pixel_columns
    )
    evolved = exchange(
        functools.partial(total_kernel, levs),
        2,
        local.shape,
        (levs - 1, blocks // levs, pixels),
        [(levs - 1,)] * 4,
        local,
    )
    live = jnp.arange(pixels, dtype=jnp.int32)[None, :] < pixel_counts[:, None]
    weight = jnp.where(live, obs_weight.astype(F32), 0.0)
    partial = call(
        functools.partial(adjoint_kernel, scale),
        (horiz, LANES, tiles * levels),
        F32,
        1,
        owner_ids,
        kernels,
        pixel_columns,
        evolved,
        innovation.astype(F32),
        weight,
    )
    partial = partial.reshape(horiz, LANES, tiles, levels).transpose(0, 3, 2, 1)
    partial = partial.reshape(horiz, levels, width)
    edge = jnp.zeros((1, levels, HALF), F32)
    after = jnp.concatenate([partial[1:, :, :HALF], edge], axis=0)
    before = jnp.concatenate([edge, partial[:-1, :, width - HALF :]], axis=0)
    blank = jnp.zeros((horiz, levels, LANES - 2 * HALF), F32)
    partial = jnp.concatenate([partial, after, before, blank], axis=2)
    fg_all = exchange(
        functools.partial(return_kernel, horiz, levs),
        3,
        (levs, levels, width + LANES),
        (horiz - 1, levels, width + LANES),
        [(horiz - 1,)] * 2 + [(levs - 1,)] * 2,
        partial,
    ).reshape(levs * levels, width + LANES)
    return call(
        final_kernel, control.shape, F32, 0, mixed_all, fg_all, kron, hi, lo, control
    )


def solution(mesh):
    placed = (
        P("lev", None, "horiz"),
        P("lev", None, None, "horiz"),
        P(),
        P("horiz", "lev", None),
        P("horiz", None),
        P("horiz", None),
        P("horiz", None),
        P("horiz", None),
        P("horiz"),
    )
    return jax.shard_map(
        body, mesh=mesh, in_specs=placed, out_specs=P("lev", None, "horiz"), check_vma=False
    )
```

```python
import functools
import math

import jax
import jax.numpy as jnp
import numpy as np
from jax import lax
from jax.experimental import pallas as pl
from jax.experimental.pallas import tpu as pltpu
from jax.sharding import PartitionSpec as P

LEV = 64
HALF = 4
LANES = 128
PAIR = 16
GROUP = 64
BF = jnp.bfloat16
F32 = jnp.float32


def level_matrix():
    index_levels = np.arange(LEV, dtype=np.float32)
    spread = np.float32(LEV / 8.0)
    distance = index_levels[:, None] - index_levels[None, :]
    matrix = np.exp(-distance * distance / (2 * spread * spread)) / (np.float32(2.5066283) * spread)
    return matrix.astype(BF)


def column_taps():
    offsets = np.arange(2 * HALF + 1, dtype=np.float32) - HALF
    spread = np.float32(HALF / 2.0)
    weights = np.exp(-offsets * offsets / (2 * spread * spread))
    return weights / np.sum(weights)


def tap_matrix(width):
    rows = np.arange(width + LANES)
    place = np.where(rows < width + HALF, rows, rows - width - 2 * HALF)
    gap = place[:, None] - np.arange(width)[None, :]
    near = (np.abs(gap) <= HALF) & (rows < width + 2 * HALF)[:, None]
    dense = np.where(near, column_taps()[np.clip(gap + HALF, 0, 2 * HALF)], 0.0).astype(np.float32)
    high = dense.astype(BF)
    low = (dense - high.astype(np.float32)).astype(BF)
    return jnp.asarray(high), jnp.asarray(low)


def spread_levels(matrix):
    dense = np.kron(matrix.astype(np.float32), np.eye(PAIR, dtype=np.float32))
    return jnp.asarray(dense.astype(BF))


def dot(a, b):
    return jnp.dot(a, b, preferred_element_type=F32)


def field_kernel(scale, all_ref, kron_ref, mixed_ref, out_ref):
    levels, members, width = mixed_ref.shape
    total = None
    for half in range(members // PAIR):
        part = pl.ds(half * PAIR, PAIR)
        x = all_ref[:, part, :].reshape(LEV * PAIR, width)
        inc = dot(kron_ref[...], x).reshape(levels, PAIR, width)
        term = jnp.sum(mixed_ref[:, part, :].astype(F32) * inc, axis=1)
        total = term if total is None else total + term
    total = total * scale
    for tile in range(width // LANES):
        out_ref[tile] = total[:, tile * LANES : (tile + 1) * LANES]


def forward_kernel(owner_ref, field_ref, kern_ref, col_ref, out_ref):
    blocks = col_ref.shape[0]
    tiles, levels = field_ref.shape[1], field_ref.shape[2]

    def step(group, carry):
        base = pl.multiple_of(group * GROUP, GROUP)
        cols = col_ref[pl.ds(base, GROUP), :]
        rows = []
        for i in range(GROUP):
            owner = owner_ref[base + i]
            col = jnp.broadcast_to(cols[i : i + 1, :], (levels, LANES))
            low = jnp.bitwise_and(col, LANES - 1)
            high = jnp.right_shift(col, 7)
            picked = jnp.take_along_axis(field_ref[owner, 0], low, axis=1)
            for tile in range(1, tiles):
                other = jnp.take_along_axis(field_ref[owner, tile], low, axis=1)
                picked = jnp.where(high == tile, other, picked)
            prod = picked * kern_ref[base + i].astype(F32)
            rows.append(jnp.sum(prod, axis=0, keepdims=True))
        out_ref[pl.ds(base, GROUP), :] = jnp.concatenate(rows, axis=0)
        return carry

    lax.fori_loop(0, blocks // GROUP, step, 0)


def adjoint_kernel(scale, owner_ref, kern_ref, col_ref, ev_ref, inn_ref, w_ref, out_ref):
    blocks = col_ref.shape[0]
    levels = kern_ref.shape[1]
    tiles = out_ref.shape[2] // levels
    out_ref[...] = jnp.zeros_like(out_ref)
    lane_row = lax.broadcasted_iota(jnp.int32, (LANES, LANES), 0).astype(F32).astype(BF)
    one, zero = jnp.ones((), BF), jnp.zeros((), BF)

    def step(group, carry):
        base = pl.multiple_of(group * GROUP, GROUP)
        cols = col_ref[pl.ds(base, GROUP), :]
        low = jnp.bitwise_and(cols, LANES - 1).astype(F32)
        high = jnp.right_shift(cols, 7)
        misfit = w_ref[pl.ds(base, GROUP), :] * (
            ev_ref[pl.ds(base, GROUP), :] - inn_ref[pl.ds(base, GROUP), :]
        )
        misfit = misfit * scale
        parts = [jnp.where(high == tile, misfit, 0.0) for tile in range(tiles)]
        for i in range(GROUP):
            owner = owner_ref[base + i]
            kern = kern_ref[base + i].astype(F32)
            rows = jnp.concatenate(
                [(kern * part[i : i + 1, :]).astype(BF) for part in parts], axis=0
            )
            row = jnp.broadcast_to(low[i : i + 1, :], (LANES, LANES)).astype(BF)
            hot = jnp.where(lane_row == row, one, zero)
            out_ref[owner] += lax.dot_general(
                hot, rows, (((1,), (1,)), ((), ())), preferred_element_type=F32
            )
        return carry

    lax.fori_loop(0, blocks // GROUP, step, 0)


def final_kernel(mixed_ref, fg_ref, kron_ref, hi_ref, lo_ref, control_ref, out_ref):
    levels, members, width = control_ref.shape
    ext = mixed_ref.shape[2]
    fg = fg_ref[...]
    for half in range(members // PAIR):
        part = pl.ds(half * PAIR, PAIR)
        grad = mixed_ref[:, part, :].astype(F32) * fg[:, None, :]
        grad = grad.reshape(LEV * PAIR, ext)
        high = grad.astype(BF)
        low = (grad - high.astype(F32)).astype(BF)
        mixed_levels = dot(kron_ref[...], high) + dot(kron_ref[...], low)
        high = mixed_levels.astype(BF)
        low = (mixed_levels - high.astype(F32)).astype(BF)
        total = dot(high, hi_ref[...]) + dot(high, lo_ref[...]) + dot(low, hi_ref[...])
        out_ref[:, part, :] = control_ref[:, part, :] + total.reshape(levels, PAIR, width)


def greet(partners):
    barrier = pltpu.get_barrier_semaphore()
    for device in partners:
        pl.semaphore_signal(barrier, inc=1, device_id=device, device_id_type=MESH)
    pl.semaphore_wait(barrier, len(partners))


def send(src, dst, send_sem, recv_sem, device):
    copy = pltpu.make_async_remote_copy(
        src_ref=src,
        dst_ref=dst,
        send_sem=send_sem,
        recv_sem=recv_sem,
        device_id=device,
        device_id_type=MESH,
    )
    copy.start()
    return copy


def others(axis, count):
    me = lax.axis_index(axis)
    return [lax.rem(me + k, count) for k in range(1, count)]


def prepare_kernel(
    count,
    ext_ref,
    control_ref,
    members_ref,
    hi_ref,
    lo_ref,
    mixed_ref,
    ext_out,
    smooth_ref,
    out_tiles,
    in_tiles,
    send_sem,
    recv_sem,
):
    levels, members, width = control_ref.shape
    me = lax.axis_index("horiz")
    right, left = lax.rem(me + 1, count), lax.rem(me + count - 1, count)
    greet([{"horiz": right}, {"horiz": left}])
    lane = lax.broadcasted_iota(jnp.int32, (levels * members, LANES), 1)

    def mix(tile):
        part = pl.ds(tile * LANES, LANES)
        total = ext_ref[0] * members_ref[:, 0, :, part].astype(F32)
        for species in range(1, members_ref.shape[1]):
            total = total + ext_ref[species] * members_ref[:, species, :, part].astype(F32)
        mixed_ref[:, :, part] = total
        ext_out[:, :, part] = total.astype(BF)
        return total.reshape(levels * members, LANES)

    def own(tile):
        return control_ref[:, :, pl.ds(tile * LANES, LANES)].reshape(levels * members, LANES)

    last = width // LANES - 1
    first_mix, last_mix = mix(0), mix(last)
    to_left = jnp.where(lane < HALF, own(0), pltpu.roll(first_mix, 8, 1))
    to_right = jnp.where(lane < 8, pltpu.roll(own(last), 8, 1), pltpu.roll(last_mix, 16, 1))
    out_tiles[0] = to_left.astype(BF)
    out_tiles[1] = to_right.astype(BF)
    copies = [
        send(out_tiles.at[k], in_tiles.at[k], send_sem.at[k], recv_sem.at[k], {"horiz": peer})
        for k, peer in enumerate((left, right))
    ]
    for tile in range(1, last):
        mix(tile)
    x = control_ref[...].astype(BF).reshape(levels * members, width)
    total = dot(x, hi_ref[pl.ds(0, width), :]) + dot(x, lo_ref[pl.ds(0, width), :])
    for copy in copies:
        copy.wait()
    after = HALF * jnp.where(me < count - 1, 1, 0)
    before = HALF * jnp.where(me > 0, 1, 0)
    bit = jnp.bitwise_and(lane, 7)
    halo = jnp.where(bit < after, in_tiles[0].astype(F32), 0.0)
    halo = jnp.where(
        (bit >= HALF) & (bit < HALF + before), in_tiles[1].astype(F32), halo
    )
    shifted = jnp.where(lane < 8, pltpu.roll(halo, LANES - 8, 1), 0.0)
    ext_out[:, :, pl.ds(width, LANES)] = shifted.astype(BF).reshape(levels, members, LANES)
    halo = jnp.where(lane < 8, halo, 0.0).astype(BF)
    total = total + dot(halo, hi_ref[pl.ds(width, LANES), :])
    total = total + dot(halo, lo_ref[pl.ds(width, LANES), :])
    smooth_ref[...] = total.astype(BF).reshape(levels, members, width)


def gather_kernel(axis, count, x_ref, out_ref, send_sem, recv_sem):
    me = lax.axis_index(axis)
    peers = others(axis, count)
    greet([{axis: peer} for peer in peers])
    copies = [
        send(x_ref, out_ref.at[me], send_sem.at[k], recv_sem.at[k], {axis: peer})
        for k, peer in enumerate(peers)
    ]
    out_ref[me] = x_ref[...]
    for copy in copies:
        copy.wait()


def level_gather_kernel(x_ref, out_ref, far_s, far_r, near_s, near_r, on_s, on_r):
    me = lax.axis_index("lev")
    near = me + 1 - 2 * lax.rem(me, 2)
    far = lax.rem(me + 2, 4)
    greet([{"lev": near}, {"lev": far}])
    chunks = far_s.shape[0]
    rows = x_ref.shape[0] // chunks
    parts = [pl.ds(c * rows, rows) for c in range(chunks)]
    away = [
        send(x_ref.at[part], out_ref.at[me, part], far_s.at[c], far_r.at[c], {"lev": far})
        for c, part in enumerate(parts)
    ]
    beside = send(x_ref, out_ref.at[me], near_s, near_r, {"lev": near})
    out_ref[me] = x_ref[...]
    onward = []
    for c, part in enumerate(parts):
        away[c].wait_recv()
        block = out_ref.at[far, part]
        onward.append(send(block, block, on_s.at[c], on_r.at[c], {"lev": near}))
    for copy in away:
        copy.wait_send()
    beside.wait()
    for copy in onward:
        copy.wait()


def total_kernel(count, x_ref, out_ref, slots, send_a, recv_a, send_b, recv_b):
    me = lax.axis_index("lev")
    peers = others("lev", count)
    greet([{"lev": peer} for peer in peers])
    rows = x_ref.shape[0] // count
    copies = [
        send(
            x_ref.at[pl.ds(pl.multiple_of(peer * rows, rows), rows)],
            slots.at[k],
            send_a.at[k],
            recv_a.at[k],
            {"lev": peer},
        )
        for k, peer in enumerate(peers)
    ]
    mine = pl.ds(pl.multiple_of(me * rows, rows), rows)
    total = x_ref[mine, :]
    for k, copy in enumerate(copies):
        copy.wait()
        total = total + slots[k]
    out_ref[mine, :] = total
    block = out_ref.at[mine]
    copies = [
        send(block, block, send_b.at[k], recv_b.at[k], {"lev": peer})
        for k, peer in enumerate(peers)
    ]
    for copy in copies:
        copy.wait()


def return_kernel(count, levs, x_ref, out_ref, slots, send_a, recv_a, send_b, recv_b):
    me, lev = lax.axis_index("horiz"), lax.axis_index("lev")
    peers = others("horiz", count)
    sides = others("lev", levs)
    greet([{"horiz": peer} for peer in peers] + [{"lev": side} for side in sides])
    copies = [
        send(x_ref.at[peer], slots.at[k], send_a.at[k], recv_a.at[k], {"horiz": peer})
        for k, peer in enumerate(peers)
    ]
    total = x_ref[me]
    for k, copy in enumerate(copies):
        copy.wait()
        total = total + slots[k]
    out_ref[lev] = total
    block = out_ref.at[lev]
    copies = [
        send(block, block, send_b.at[k], recv_b.at[k], {"lev": side})
        for k, side in enumerate(sides)
    ]
    for copy in copies:
        copy.wait()


def vmem(count):
    return [pl.BlockSpec(memory_space=pltpu.VMEM)] * count


def smem(count):
    return [pl.BlockSpec(memory_space=pltpu.SMEM)] * count


MESH = pl.DeviceIdType.MESH
PARAMS = pltpu.CompilerParams(vmem_limit_bytes=48 * 1024 * 1024)


def call(kernel, shape, dtype, scalars, *args):
    return pl.pallas_call(
        kernel,
        out_shape=jax.ShapeDtypeStruct(shape, dtype),
        in_specs=smem(scalars) + vmem(len(args) - scalars),
        out_specs=pl.BlockSpec(memory_space=pltpu.VMEM),
        compiler_params=PARAMS,
    )(*args)


def exchange(kernel, number, shape, slots, sems, x):
    scratch = [pltpu.VMEM(slots, F32)] if slots else []
    scratch += [pltpu.SemaphoreType.DMA(size) for size in sems]
    return pl.pallas_call(
        kernel,
        out_shape=jax.ShapeDtypeStruct(shape, x.dtype),
        in_specs=vmem(1),
        out_specs=pl.BlockSpec(memory_space=pltpu.VMEM),
        scratch_shapes=scratch,
        compiler_params=pltpu.CompilerParams(
            vmem_limit_bytes=32 * 1024 * 1024, collective_id=number, has_side_effects=True
        ),
    )(x)


def body(
    control,
    members,
    extinction,
    kernels,
    innovation,
    obs_weight,
    owners,
    pixel_columns,
    pixel_counts,
):
    levels, mem_count, width = control.shape
    blocks, _, pixels = kernels.shape
    horiz = lax.axis_size("horiz")
    tiles = width // LANES
    level_loc = level_matrix()
    first = lax.axis_index("lev") * levels
    kron = lax.dynamic_slice_in_dim(
        spread_levels(level_loc), first * PAIR, levels * PAIR, 0
    )
    levs = lax.axis_size("lev")
    hi, lo = tap_matrix(width)
    scale = 1.0 / math.sqrt(mem_count)
    owner_ids = owners[:, 0]

    strip = (levels, mem_count, width)
    edge_tiles = pltpu.VMEM((2, levels * mem_count, LANES), BF)
    mixed, mixed_ext, smooth = pl.pallas_call(
        functools.partial(prepare_kernel, horiz),
        out_shape=[
            jax.ShapeDtypeStruct(strip, F32),
            jax.ShapeDtypeStruct((levels, mem_count, width + LANES), BF),
            jax.ShapeDtypeStruct(strip, BF),
        ],
        in_specs=smem(1) + vmem(4),
        out_specs=vmem(3),
        scratch_shapes=[edge_tiles, edge_tiles] + [pltpu.SemaphoreType.DMA((2,))] * 2,
        compiler_params=pltpu.CompilerParams(
            vmem_limit_bytes=40 * 1024 * 1024, collective_id=4, has_side_effects=True
        ),
    )(extinction, control, members, hi, lo)
    smooth_all = exchange(
        level_gather_kernel,
        0,
        (levs,) + smooth.shape,
        None,
        [(8,), (8,), (), (), (8,), (8,)],
        smooth,
    ).reshape((levs * levels,) + smooth.shape[1:])

    smooth_all, mixed_ext = lax.optimization_barrier((smooth_all, mixed_ext))
    mixed_all = lax.all_gather(mixed_ext, "lev", axis=0, tiled=True)

    field = call(
        functools.partial(field_kernel, scale),
        (tiles, levels, LANES),
        F32,
        0,
        smooth_all,
        kron,
        mixed,
    )
    field_all = exchange(
        functools.partial(gather_kernel, "horiz", horiz),
        1,
        (horiz,) + field.shape,
        None,
        [(horiz - 1,)] * 2,
        field,
    )
    local = call(
        forward_kernel, (blocks, pixels), F32, 1, owner_ids, field_all, kernels, pixel_columns
    )
    evolved = exchange(
        functools.partial(total_kernel, levs),
        2,
        local.shape,
        (levs - 1, blocks // levs, pixels),
        [(levs - 1,)] * 4,
        local,
    )
    live = jnp.arange(pixels, dtype=jnp.int32)[None, :] < pixel_counts[:, None]
    weight = jnp.where(live, obs_weight.astype(F32), 0.0)
    partial = call(
        functools.partial(adjoint_kernel, scale),
        (horiz, LANES, tiles * levels),
        F32,
        1,
        owner_ids,
        kernels,
        pixel_columns,
        evolved,
        innovation.astype(F32),
        weight,
    )
    partial = partial.reshape(horiz, LANES, tiles, levels).transpose(0, 3, 2, 1)
    partial = partial.reshape(horiz, levels, width)
    edge = jnp.zeros((1, levels, HALF), F32)
    after = jnp.concatenate([partial[1:, :, :HALF], edge], axis=0)
    before = jnp.concatenate([edge, partial[:-1, :, width - HALF :]], axis=0)
    blank = jnp.zeros((horiz, levels, LANES - 2 * HALF), F32)
    partial = jnp.concatenate([partial, after, before, blank], axis=2)
    fg_all = exchange(
        functools.partial(return_kernel, horiz, levs),
        3,
        (levs, levels, width + LANES),
        (horiz - 1, levels, width + LANES),
        [(horiz - 1,)] * 2 + [(levs - 1,)] * 2,
        partial,
    ).reshape(levs * levels, width + LANES)
    return call(
        final_kernel, control.shape, F32, 0, mixed_all, fg_all, kron, hi, lo, control
    )


def solution(mesh):
    placed = (
        P("lev", None, "horiz"),
        P("lev", None, None, "horiz"),
        P(),
        P("horiz", "lev", None),
        P("horiz", None),
        P("horiz", None),
        P("horiz", None),
        P("horiz", None),
        P("horiz"),
    )
    return jax.shard_map(
        body, mesh=mesh, in_specs=placed, out_specs=P("lev", None, "horiz"), check_vma=False
    )
```
